512 devices in a mesh: dp: 128 (over y, z, core), fsdp: 4 (over x).
Axes of the slice: x: 4, y: 8, z: 8, core: 2. Of those that a mesh axis runs over, the one named last changes fastest.
Arguments:
- inputs: bfloat16 [49152, 2560], P('dp', 'fsdp'), may hold values from -6 to 6
- out_grad: bfloat16 [49152, 2560], P('dp', 'fsdp'), may hold values from -0.0625 to 0.0625
- basis: bfloat16 [2560, 512], P('fsdp'), may hold values from -0.25 to 0.25
- moment_first: float32 [512, 2560], P('dp', 'fsdp'), may hold values from -1.5 to 1.5
- moment_second: float32 [512, 2560], P('dp', 'fsdp'), may hold values from 0.0002 to 0.004
Outputs:
- update: bfloat16 [2560, 2560], P('fsdp')
- new_first: float32 [512, 2560], P('dp', 'fsdp')
- new_second: float32 [512, 2560], P('dp', 'fsdp')
The draws below stay inside these ranges and needn't reach their ends.
All inputs are finite; a program needn't handle non-finite values.
Results may differ from the reference program's by a relative error of at most 0.0063.
Values may be sent and summed in bfloat16 or wider, within the bound.
No kernel may reach another device: no remote copies, remote signals or barrier semaphores. Data moves between devices by JAX's collectives and lax.ppermute only.
A program may use at most 64 MiB of HBM per device.

```python
import math
import jax
import jax.numpy as jnp

DIN = 2560
DOUT = 2560
RANK = 512
STEP = 10
TOKENS = 49152


def block_scale(key, shape, shards, low, largest):
    loudness = 1.0
    for dim, shards_of in shards:
        draws = jax.random.uniform(jax.random.fold_in(jax.random.fold_in(key, 6), dim), (shards_of,), jnp.float32, low / len(shards), largest / len(shards))
        loudness = loudness * jnp.repeat(jnp.exp(draws), shape[dim] // shards_of).reshape((-1,) + (1,) * (len(shape) - 1 - dim))
    return loudness


def gaussian(own_key, dims, scale, most, pieces=(), kind=jnp.bfloat16):
    result = jax.random.normal(own_key, dims, jnp.float32) * scale
    if len(pieces) > 0:
        result = block_scale(own_key, dims, pieces, -0.22, 0.18) * result
    return jnp.clip(result, min=-most, max=most).astype(kind)


def setup_inputs(seed: int = 0) -> dict:
    key_list = jax.random.split(jax.random.key(seed), 6)
    inputs = gaussian(key_list[0], (TOKENS, DIN), 1.0, 6.0, ((0, 128), (1, 4)))
    out_grad = gaussian(key_list[1], (TOKENS, DOUT), (TOKENS ** -0.5), 0.0625, ((0, 128), (1, 4)))
    basis = gaussian(key_list[2], (DIN, RANK), RANK ** -0.5, 0.25, ((0, 4),))
    moment_first = gaussian(key_list[3], (RANK, DOUT), 0.1, 1.5, ((0, 128), (1, 4)), jnp.float32)
    moment_second = jnp.clip(jnp.exp(math.log(0.004) - 2.9957323 * jax.random.uniform(key_list[4], (RANK, DOUT), jnp.float32) ** block_scale(key_list[4], (RANK, DOUT), ((0, 128), (1, 4)), -0.2, 0.2)), 0.0002, 0.004)
    return dict(inputs=inputs, out_grad=out_grad, basis=basis, moment_first=moment_first, moment_second=moment_second)


def reference(inputs, out_grad, basis, moment_first, moment_second):
    projected_in = jnp.dot(inputs, basis, preferred_element_type=jnp.float32).astype(jnp.bfloat16)
    grad_proj = jnp.dot(projected_in.T, out_grad, preferred_element_type=jnp.float32)
    new_first = 0.9 * moment_first + 0.1 * grad_proj
    new_second = 0.999 * moment_second + 0.001 * grad_proj * grad_proj
    corrected = new_first / (1.0 - 0.9 ** STEP)
    scaled = jnp.sqrt(new_second / (1.0 - 0.999 ** STEP)) + 1e-08
    direction = (corrected / scaled).astype(jnp.bfloat16)
    update = jnp.dot(basis, direction, preferred_element_type=jnp.float32).astype(jnp.bfloat16)
    return (update, new_first, new_second)
```

```python
import jax
import jax.numpy as jnp
from jax import lax
from jax.sharding import Mesh, PartitionSpec as P

STEP = 10
F32 = jnp.float32
BF16 = jnp.bfloat16


def spread(block, axes, n):
    return lax.all_to_all(jnp.broadcast_to(block[None], (n,) + block.shape), axes, 0, 0)


def per_device(ny, nz, nx, inputs, out_grad, basis, moment_first, moment_second):
    rank = basis.shape[1]
    groups = ny * nz
    own = moment_first.shape[0]
    half = rank // 2
    core = lax.axis_index("c")

    old = lax.broadcasted_iota(jnp.int32, (rank, rank), 0)
    new = lax.broadcasted_iota(jnp.int32, (rank, rank), 1)
    side = (new // half + core) % 2
    wanted = (new % half) // own * (2 * own) + side * own + new % own
    basis = jnp.dot(basis, (old == wanted).astype(BF16), preferred_element_type=F32).astype(BF16)

    partial = jnp.dot(inputs, basis, preferred_element_type=F32).astype(BF16)
    parts = spread(partial, "x", nx)
    projected = jnp.sum(parts.astype(F32), axis=0).astype(BF16)
    grad = lax.dot_general(projected, out_grad, (((0,), (0,)), ((), ())), preferred_element_type=F32)

    swap = [(0, 1), (1, 0)]
    theirs = lax.ppermute(grad[half:], "c", swap)
    chip = (grad[:half] + theirs).astype(BF16).reshape(groups, own, -1)
    grad_shard = jnp.sum(lax.all_to_all(chip, ("y", "z"), 0, 0).astype(F32), axis=0)

    new_first = 0.9 * moment_first + 0.1 * grad_shard
    new_second = 0.999 * moment_second + 0.001 * grad_shard * grad_shard
    corrected = new_first / (1.0 - 0.9**STEP)
    scaled = jnp.sqrt(new_second / (1.0 - 0.999**STEP)) + 1e-08
    direction = (corrected / scaled).astype(BF16)

    rows = spread(direction, ("y", "z"), groups).reshape(half, -1)
    mine = spread(rows, "x", nx)
    other = lax.ppermute(mine, "c", swap)
    update = [
        (
            jnp.dot(basis[:, :half], mine[i], preferred_element_type=F32)
            + jnp.dot(basis[:, half:], other[i], preferred_element_type=F32)
        ).astype(BF16)
        for i in range(nx)
    ]
    return (jnp.concatenate(update, axis=1), new_first, new_second)


def solution(mesh):
    ny, nz, nx = 8, 8, mesh.devices.shape[1]
    split = Mesh(mesh.devices.reshape(ny, nz, 2, nx), ("y", "z", "c", "x"))
    dp = ("y", "z", "c")

    def body(*args):
        return per_device(ny, nz, nx, *args)

    return jax.shard_map(
        body,
        mesh=split,
        in_specs=(P(dp, "x"), P(dp, "x"), P("x", None), P(dp, "x"), P(dp, "x")),
        out_specs=(P("x", None), P(dp, "x"), P(dp, "x")),
        check_vma=False,
    )
```

```python
import jax
import jax.numpy as jnp
from jax import lax
from jax.experimental import pallas as pl
from jax.experimental.pallas import tpu as pltpu
from jax.sharding import Mesh, PartitionSpec as P

STEP = 10
F32 = jnp.float32
BF16 = jnp.bfloat16


def spread(block, axes, n):
    return lax.all_to_all(jnp.broadcast_to(block[None], (n,) + block.shape), axes, 0, 0)


def rank_order(rank, own, first):
    half = rank // 2
    old = lax.broadcasted_iota(jnp.int32, (rank, rank), 0)
    new = lax.broadcasted_iota(jnp.int32, (rank, rank), 1)
    side = (new // half + first) % 2
    return (old == (new % half) // own * (2 * own) + side * own + new % own).astype(BF16)


def expand_kernel(basis_ref, mine_ref, other_ref, out_ref):
    half = mine_ref.shape[0]
    acc = jnp.dot(basis_ref[:, :half], mine_ref[...], preferred_element_type=F32)
    acc += jnp.dot(basis_ref[:, half:], other_ref[...], preferred_element_type=F32)
    out_ref[...] = acc.astype(out_ref.dtype)


def expand(basis, mine, other):
    nx, half, cols = mine.shape
    rows = basis.shape[0]
    return pl.pallas_call(
        expand_kernel,
        grid=(nx,),
        in_specs=[
            pl.BlockSpec((rows, 2 * half), lambda i: (0, 0)),
            pl.BlockSpec((None, half, cols), lambda i: (i, 0, 0)),
            pl.BlockSpec((None, half, cols), lambda i: (i, 0, 0)),
        ],
        out_specs=pl.BlockSpec((rows, cols), lambda i: (0, i)),
        out_shape=jax.ShapeDtypeStruct((rows, nx * cols), BF16),
        compiler_params=pltpu.CompilerParams(vmem_limit_bytes=24 * 1024 * 1024),
        cost_estimate=pl.CostEstimate(
            flops=4 * rows * half * nx * cols, bytes_accessed=10 * 1024 * 1024, transcendentals=0
        ),
    )(basis, mine, other)


def per_device(ny, nz, nx, inputs, out_grad, basis, moment_first, moment_second):
    rank = basis.shape[1]
    tokens = inputs.shape[0]
    groups = ny * nz
    own, cols = moment_first.shape
    half = rank // 2
    core = lax.axis_index("c")
    swap = [(0, 1), (1, 0)]

    partial = jnp.dot(inputs, basis, preferred_element_type=F32).astype(BF16)
    parts = lax.all_to_all(partial.reshape(nx, tokens // nx, rank), "x", 0, 0)

    theirs = lax.ppermute(out_grad, "c", swap)
    grads = jnp.where(
        core == 0, jnp.concatenate([out_grad, theirs]), jnp.concatenate([theirs, out_grad])
    )
    basis = jnp.dot(basis, rank_order(rank, own, core), preferred_element_type=F32).astype(BF16)

    projected = jnp.sum(parts.astype(F32), axis=0).astype(BF16)
    ordered = jnp.dot(projected, rank_order(rank, own, 0), preferred_element_type=F32).astype(BF16)
    sides = ordered.reshape(tokens // nx, 2, half).transpose(1, 0, 2)
    sides = jnp.broadcast_to(sides[:, None], (2, nx, tokens // nx, half)).reshape(2 * nx, tokens // nx, half)
    rows = lax.all_to_all(sides, ("c", "x"), 0, 0).reshape(2 * tokens, half)
    chip = lax.dot_general(rows, grads, (((0,), (0,)), ((), ())), preferred_element_type=F32)
    chip = chip.astype(BF16).reshape(groups, own, cols)
    grad_shard = jnp.sum(lax.all_to_all(chip, ("y", "z"), 0, 0).astype(F32), axis=0)

    new_first = 0.9 * moment_first + 0.1 * grad_shard
    new_second = 0.999 * moment_second + 0.001 * grad_shard * grad_shard
    corrected = new_first / (1.0 - 0.9**STEP)
    scaled = jnp.sqrt(new_second / (1.0 - 0.999**STEP)) + 1e-08
    direction = (corrected / scaled).astype(BF16)

    gathered = spread(direction, ("y", "z"), groups).reshape(half, cols)
    mine = spread(gathered, "x", nx)
    other = lax.ppermute(mine, "c", swap)
    return (expand(basis, mine, other), new_first, new_second)


def solution(mesh):
    ny, nz, nx = 8, 8, mesh.devices.shape[1]
    split = Mesh(mesh.devices.reshape(ny, nz, 2, nx), ("y", "z", "c", "x"))
    dp = ("y", "z", "c")

    def body(*args):
        return per_device(ny, nz, nx, *args)

    return jax.shard_map(
        body,
        mesh=split,
        in_specs=(P(dp, "x"), P(dp, "x"), P("x", None), P(dp, "x"), P(dp, "x")),
        out_specs=(P("x", None), P(dp, "x"), P(dp, "x")),
        check_vma=False,
    )
```

```python
import functools

import jax
import jax.numpy as jnp
from jax import lax
from jax.experimental import pallas as pl
from jax.experimental.pallas import tpu as pltpu
from jax.sharding import Mesh, PartitionSpec as P

STEP = 10
F32 = jnp.float32
BF16 = jnp.bfloat16


def spread(block, axes, n):
    return lax.all_to_all(jnp.broadcast_to(block[None], (n,) + block.shape), axes, 0, 0)


def rank_order(rank, own, first):
    half = rank // 2
    old = lax.broadcasted_iota(jnp.int32, (rank, rank), 0)
    new = lax.broadcasted_iota(jnp.int32, (rank, rank), 1)
    side = (new // half + first) % 2
    return (old == (new % half) // own * (2 * own) + side * own + new % own).astype(BF16)


def whole():
    return pl.BlockSpec(memory_space=pltpu.VMEM)


def project_kernel(inputs_ref, basis_ref, out_ref):
    out_ref[...] = jnp.dot(inputs_ref[...], basis_ref[...], preferred_element_type=F32).astype(BF16)


def project(inputs, basis):
    return pl.pallas_call(
        project_kernel,
        in_specs=[whole(), whole()],
        out_specs=whole(),
        out_shape=jax.ShapeDtypeStruct((inputs.shape[0], basis.shape[1]), BF16),
        compiler_params=pltpu.CompilerParams(vmem_limit_bytes=16 * 1024 * 1024),
    )(inputs, basis)


def combine_kernel(own, parts_ref, out_ref):
    nx, _, rank = parts_ref.shape
    half = rank // 2
    total = parts_ref[0].astype(F32)
    for i in range(1, nx):
        total += parts_ref[i].astype(F32)
    total = total.astype(BF16)
    old = lax.broadcasted_iota(jnp.int32, (rank, half), 0)
    new = lax.broadcasted_iota(jnp.int32, (rank, half), 1)
    for c in range(2):
        pick = (old == new // own * (2 * own) + c * own + new % own).astype(F32).astype(BF16)
        side = jnp.dot(total, pick, preferred_element_type=F32).astype(BF16)
        for i in range(nx):
            out_ref[c * nx + i] = side


def combine(parts, own):
    nx, tokens, rank = parts.shape
    return pl.pallas_call(
        functools.partial(combine_kernel, own),
        in_specs=[whole()],
        out_specs=whole(),
        out_shape=jax.ShapeDtypeStruct((2 * nx, tokens, rank // 2), BF16),
        compiler_params=pltpu.CompilerParams(vmem_limit_bytes=16 * 1024 * 1024),
    )(parts)


def expand_mine_kernel(basis_ref, mine_ref, out_ref):
    nx, half, _ = mine_ref.shape
    for i in range(nx):
        out_ref[i] = jnp.dot(basis_ref[:, :half], mine_ref[i], preferred_element_type=F32)


def expand_mine(basis, mine):
    nx, half, cols = mine.shape
    rows = basis.shape[0]
    return pl.pallas_call(
        expand_mine_kernel,
        in_specs=[whole(), whole()],
        out_specs=whole(),
        out_shape=jax.ShapeDtypeStruct((nx, rows, cols), F32),
        compiler_params=pltpu.CompilerParams(vmem_limit_bytes=24 * 1024 * 1024),
        cost_estimate=pl.CostEstimate(
            flops=2 * rows * half * nx * cols, bytes_accessed=4 * nx * rows * cols, transcendentals=0
        ),
    )(basis, mine)


def expand_kernel(tiles, basis_ref, other_ref, mine_ref, out_ref, done, sems):
    nx, half, cols = other_ref.shape
    size = basis_ref.shape[0] // tiles
    copies = []
    for t in range(tiles):
        rows = pl.ds(t * size, size)
        for i in range(nx):
            acc = mine_ref[i, rows, :] + jnp.dot(
                basis_ref[rows, half:], other_ref[i], preferred_element_type=F32
            )
            done[rows, pl.ds(i * cols, cols)] = acc.astype(BF16)
        copies.append(pltpu.make_async_copy(done.at[rows], out_ref.at[rows], sems.at[t]))
        copies[-1].start()
    for copy in copies:
        copy.wait()


def expand(basis, other, mine, tiles=5):
    nx, half, cols = other.shape
    rows = basis.shape[0]
    return pl.pallas_call(
        functools.partial(expand_kernel, tiles),
        in_specs=[whole(), whole(), whole()],
        out_specs=pl.BlockSpec(memory_space=pl.ANY),
        out_shape=jax.ShapeDtypeStruct((rows, nx * cols), BF16),
        scratch_shapes=[pltpu.VMEM((rows, nx * cols), BF16), pltpu.SemaphoreType.DMA((tiles,))],
        compiler_params=pltpu.CompilerParams(vmem_limit_bytes=24 * 1024 * 1024),
    )(basis, other, mine)


def per_device(ny, nz, nx, inputs, out_grad, basis, moment_first, moment_second):
    rank = basis.shape[1]
    tokens = inputs.shape[0]
    groups = ny * nz
    own, cols = moment_first.shape
    half = rank // 2
    core = lax.axis_index("c")
    swap = [(0, 1), (1, 0)]

    partial = project(inputs, basis)
    parts = lax.all_to_all(partial.reshape(nx, tokens // nx, rank), "x", 0, 0)

    theirs = lax.ppermute(out_grad, "c", swap)
    grads = jnp.where(
        core == 0, jnp.concatenate([out_grad, theirs]), jnp.concatenate([theirs, out_grad])
    )
    basis = jnp.dot(basis, rank_order(rank, own, core), preferred_element_type=F32).astype(BF16)
    sides, basis = lax.optimization_barrier((combine(parts, own), basis))
    rows = lax.all_to_all(sides, ("c", "x"), 0, 0).reshape(2 * tokens, half)
    chip = lax.dot_general(rows, grads, (((0,), (0,)), ((), ())), preferred_element_type=F32)
    chip = chip.astype(BF16).reshape(groups, own, cols)
    grad_shard = jnp.sum(lax.all_to_all(chip, ("y", "z"), 0, 0).astype(F32), axis=0)

    new_first = 0.9 * moment_first + 0.1 * grad_shard
    new_second = 0.999 * moment_second + 0.001 * grad_shard * grad_shard
    corrected = new_first / (1.0 - 0.9**STEP)
    scaled = jnp.sqrt(new_second / (1.0 - 0.999**STEP)) + 1e-08
    direction = (corrected / scaled).astype(BF16)

    gathered = spread(direction, ("y", "z"), groups).reshape(half, cols)
    mine = spread(gathered, "x", nx)
    other = lax.ppermute(mine, "c", swap)
    return (expand(basis, other, expand_mine(basis, mine)), new_first, new_second)


def solution(mesh):
    ny, nz, nx = 8, 8, mesh.devices.shape[1]
    split = Mesh(mesh.devices.reshape(ny, nz, 2, nx), ("y", "z", "c", "x"))
    dp = ("y", "z", "c")

    def body(*args):
        return per_device(ny, nz, nx, *args)

    return jax.shard_map(
        body,
        mesh=split,
        in_specs=(P(dp, "x"), P(dp, "x"), P("x", None), P(dp, "x"), P(dp, "x")),
        out_specs=(P("x", None), P(dp, "x"), P(dp, "x")),
        check_vma=False,
    )
```

```python
import functools

import jax
import jax.numpy as jnp
from jax import lax
from jax.experimental import pallas as pl
from jax.experimental.pallas import tpu as pltpu
from jax.sharding import Mesh, PartitionSpec as P

STEP = 10
F32 = jnp.float32
BF16 = jnp.bfloat16


def spread(block, axes, n):
    return lax.all_to_all(jnp.broadcast_to(block[None], (n,) + block.shape), axes, 0, 0)


def whole():
    return pl.BlockSpec(memory_space=pltpu.VMEM)


def order_kernel(own, out_ref):
    _, rank, half = out_ref.shape
    old = lax.broadcasted_iota(jnp.int32, (rank, half), 0)
    new = lax.broadcasted_iota(jnp.int32, (rank, half), 1)
    for c in range(2):
        out_ref[c] = (old == new // own * (2 * own) + c * own + new % own).astype(F32).astype(BF16)


def rank_order(rank, own):
    return pl.pallas_call(
        functools.partial(order_kernel, own),
        in_specs=[],
        out_specs=whole(),
        out_shape=jax.ShapeDtypeStruct((2, rank, rank // 2), BF16),
        compiler_params=pltpu.CompilerParams(vmem_limit_bytes=16 * 1024 * 1024),
        cost_estimate=pl.CostEstimate(flops=4 * 10**9, bytes_accessed=8 * 10**6, transcendentals=0),
    )()


def project_kernel(inputs_ref, basis_ref, picks_ref, out_ref):
    del picks_ref
    out_ref[...] = jnp.dot(inputs_ref[...], basis_ref[...], preferred_element_type=F32).astype(BF16)


def project(inputs, basis, picks):
    return pl.pallas_call(
        project_kernel,
        in_specs=[whole(), whole(), whole()],
        out_specs=whole(),
        out_shape=jax.ShapeDtypeStruct((inputs.shape[0], basis.shape[1]), BF16),
        compiler_params=pltpu.CompilerParams(vmem_limit_bytes=16 * 1024 * 1024),
    )(inputs, basis, picks)


def combine_kernel(parts_ref, picks_ref, out_ref):
    nx = parts_ref.shape[0]
    total = parts_ref[0].astype(F32)
    for i in range(1, nx):
        total += parts_ref[i].astype(F32)
    total = total.astype(BF16)
    for c in range(2):
        side = jnp.dot(total, picks_ref[c], preferred_element_type=F32).astype(BF16)
        for i in range(nx):
            out_ref[c * nx + i] = side


def combine(parts, picks):
    nx, tokens, rank = parts.shape
    return pl.pallas_call(
        combine_kernel,
        in_specs=[whole(), whole()],
        out_specs=whole(),
        out_shape=jax.ShapeDtypeStruct((2 * nx, tokens, rank // 2), BF16),
        compiler_params=pltpu.CompilerParams(vmem_limit_bytes=16 * 1024 * 1024),
    )(parts, picks)


def project_grad_kernel(rows_ref, own_ref, theirs_ref, out_ref):
    core = lax.axis_index("c")
    total = lax.dot_general(
        rows_ref[core], own_ref[...], (((0,), (0,)), ((), ())), preferred_element_type=F32
    )
    total += lax.dot_general(
        rows_ref[1 - core], theirs_ref[...], (((0,), (0,)), ((), ())), preferred_element_type=F32
    )
    out_ref[...] = total.astype(BF16)


def project_grad(rows, own, theirs):
    return pl.pallas_call(
        project_grad_kernel,
        in_specs=[whole(), whole(), whole()],
        out_specs=whole(),
        out_shape=jax.ShapeDtypeStruct((rows.shape[2], own.shape[1]), BF16),
        compiler_params=pltpu.CompilerParams(vmem_limit_bytes=16 * 1024 * 1024),
    )(rows, own, theirs)


def expand_mine_kernel(basis_ref, picks_ref, mine_ref, out_ref, ordered_ref):
    nx, half, _ = mine_ref.shape
    core = lax.axis_index("c")
    for h in range(2):
        pick = picks_ref[core if h == 0 else 1 - core]
        ordered_ref[:, h * half : (h + 1) * half] = jnp.dot(
            basis_ref[...], pick, preferred_element_type=F32
        ).astype(BF16)
    for i in range(nx):
        out_ref[i] = jnp.dot(ordered_ref[:, :half], mine_ref[i], preferred_element_type=F32)


def expand_mine(basis, picks, mine):
    nx, half, cols = mine.shape
    rows = basis.shape[0]
    return pl.pallas_call(
        expand_mine_kernel,
        in_specs=[whole(), whole(), whole()],
        out_specs=[whole(), whole()],
        out_shape=[
            jax.ShapeDtypeStruct((nx, rows, cols), F32),
            jax.ShapeDtypeStruct(basis.shape, BF16),
        ],
        compiler_params=pltpu.CompilerParams(vmem_limit_bytes=24 * 1024 * 1024),
        cost_estimate=pl.CostEstimate(
            flops=2 * rows * half * nx * cols, bytes_accessed=4 * nx * rows * cols, transcendentals=0
        ),
    )(basis, picks, mine)


def expand_kernel(tiles, basis_ref, other_ref, mine_ref, out_ref, done, sems):
    nx, half, cols = other_ref.shape
    size = basis_ref.shape[0] // tiles
    copies = []
    for t in range(tiles):
        rows = pl.ds(t * size, size)
        for i in range(nx):
            acc = mine_ref[i, rows, :] + jnp.dot(
                basis_ref[rows, half:], other_ref[i], preferred_element_type=F32
            )
            done[rows, pl.ds(i * cols, cols)] = acc.astype(BF16)
        copies.append(pltpu.make_async_copy(done.at[rows], out_ref.at[rows], sems.at[t]))
        copies[-1].start()
    for copy in copies:
        copy.wait()


def expand(basis, other, mine, tiles=5):
    nx, half, cols = other.shape
    rows = basis.shape[0]
    return pl.pallas_call(
        functools.partial(expand_kernel, tiles),
        in_specs=[whole(), whole(), whole()],
        out_specs=pl.BlockSpec(memory_space=pl.ANY),
        out_shape=jax.ShapeDtypeStruct((rows, nx * cols), BF16),
        scratch_shapes=[pltpu.VMEM((rows, nx * cols), BF16), pltpu.SemaphoreType.DMA((tiles,))],
        compiler_params=pltpu.CompilerParams(vmem_limit_bytes=24 * 1024 * 1024),
    )(basis, other, mine)


def per_device(ny, nz, nx, inputs, out_grad, basis, moment_first, moment_second):
    rank = basis.shape[1]
    tokens = inputs.shape[0]
    groups = ny * nz
    own, cols = moment_first.shape
    half = rank // 2
    swap = [(0, 1), (1, 0)]

    theirs = lax.ppermute(out_grad, "c", swap)
    picks = rank_order(rank, own)
    partial = project(inputs, basis, picks)
    parts = lax.all_to_all(partial.reshape(nx, tokens // nx, rank), "x", 0, 0)

    sides, theirs = lax.optimization_barrier((combine(parts, picks), theirs))
    rows = lax.all_to_all(sides, ("c", "x"), 0, 0).reshape(2, tokens, half)
    chip = project_grad(rows, out_grad, theirs).reshape(groups, own, cols)
    grad_shard = jnp.sum(lax.all_to_all(chip, ("y", "z"), 0, 0).astype(F32), axis=0)

    new_first = 0.9 * moment_first + 0.1 * grad_shard
    new_second = 0.999 * moment_second + 0.001 * grad_shard * grad_shard
    corrected = new_first / (1.0 - 0.9**STEP)
    scaled = jnp.sqrt(new_second / (1.0 - 0.999**STEP)) + 1e-08
    direction = (corrected / scaled).astype(BF16)

    gathered = spread(direction, ("y", "z"), groups).reshape(half, cols)
    mine = spread(gathered, "x", nx)
    other = lax.ppermute(mine, "c", swap)
    done, ordered = expand_mine(basis, picks, mine)
    return (expand(ordered, other, done), new_first, new_second)


def solution(mesh):
    ny, nz, nx = 8, 8, mesh.devices.shape[1]
    split = Mesh(mesh.devices.reshape(ny, nz, 2, nx), ("y", "z", "c", "x"))
    dp = ("y", "z", "c")

    def body(*args):
        return per_device(ny, nz, nx, *args)

    return jax.shard_map(
        body,
        mesh=split,
        in_specs=(P(dp, "x"), P(dp, "x"), P("x", None), P(dp, "x"), P(dp, "x")),
        out_specs=(P("x", None), P(dp, "x"), P(dp, "x")),
        check_vma=False,
    )
```

```python
import functools

import jax
import jax.numpy as jnp
from jax import lax
from jax.experimental import pallas as pl
from jax.experimental.pallas import tpu as pltpu
from jax.sharding import Mesh, PartitionSpec as P

STEP = 10
F32 = jnp.float32
BF16 = jnp.bfloat16


def spread(block, axes, n):
    return lax.all_to_all(jnp.broadcast_to(block[None], (n,) + block.shape), axes, 0, 0)


def whole():
    return pl.BlockSpec(memory_space=pltpu.VMEM)


def order_kernel(own, ny, nz, out_ref):
    _, rank, half = out_ref.shape
    old = lax.broadcasted_iota(jnp.int32, (rank, half), 0)
    new = lax.broadcasted_iota(jnp.int32, (rank, half), 1)
    block = new // own
    pair = block % (nz // 2)
    y = block // (nz // 2) % ny
    parity = block // (nz // 2 * ny)
    first = ((y * nz + pair * 2 + parity) * 2) * own + new % own
    for c in range(2):
        out_ref[c] = (old == first + c * own).astype(F32).astype(BF16)


def rank_order(rank, own, ny, nz):
    return pl.pallas_call(
        functools.partial(order_kernel, own, ny, nz),
        in_specs=[],
        out_specs=whole(),
        out_shape=jax.ShapeDtypeStruct((2, rank, rank // 2), BF16),
        compiler_params=pltpu.CompilerParams(vmem_limit_bytes=16 * 1024 * 1024),
        cost_estimate=pl.CostEstimate(flops=4 * 10**9, bytes_accessed=8 * 10**6, transcendentals=0),
    )()


def project_kernel(inputs_ref, basis_ref, picks_ref, out_ref):
    del picks_ref
    out_ref[...] = jnp.dot(inputs_ref[...], basis_ref[...], preferred_element_type=F32).astype(BF16)


def project(inputs, basis, picks):
    return pl.pallas_call(
        project_kernel,
        in_specs=[whole(), whole(), whole()],
        out_specs=whole(),
        out_shape=jax.ShapeDtypeStruct((inputs.shape[0], basis.shape[1]), BF16),
        compiler_params=pltpu.CompilerParams(vmem_limit_bytes=16 * 1024 * 1024),
    )(inputs, basis, picks)


def combine_kernel(parts_ref, picks_ref, out_ref):
    nx = parts_ref.shape[0]
    total = parts_ref[0].astype(F32)
    for i in range(1, nx):
        total += parts_ref[i].astype(F32)
    total = total.astype(BF16)
    for c in range(2):
        side = jnp.dot(total, picks_ref[c], preferred_element_type=F32).astype(BF16)
        for i in range(nx):
            out_ref[c * nx + i] = side


def combine(parts, picks):
    nx, tokens, rank = parts.shape
    return pl.pallas_call(
        combine_kernel,
        in_specs=[whole(), whole()],
        out_specs=whole(),
        out_shape=jax.ShapeDtypeStruct((2 * nx, tokens, rank // 2), BF16),
        compiler_params=pltpu.CompilerParams(vmem_limit_bytes=16 * 1024 * 1024),
    )(parts, picks)


def project_grad_kernel(rows_ref, own_ref, theirs_ref, out_ref):
    core = lax.axis_index("c")
    total = lax.dot_general(
        rows_ref[core], own_ref[...], (((0,), (0,)), ((), ())), preferred_element_type=F32
    )
    total += lax.dot_general(
        rows_ref[1 - core], theirs_ref[...], (((0,), (0,)), ((), ())), preferred_element_type=F32
    )
    out_ref[...] = total.astype(BF16)


def project_grad(rows, own, theirs):
    return pl.pallas_call(
        project_grad_kernel,
        in_specs=[whole(), whole(), whole()],
        out_specs=whole(),
        out_shape=jax.ShapeDtypeStruct((rows.shape[2], own.shape[1]), BF16),
        compiler_params=pltpu.CompilerParams(vmem_limit_bytes=16 * 1024 * 1024),
    )(rows, own, theirs)


def direction_kernel(parts_ref, first_ref, second_ref, grad_ref, out_ref):
    grad = jnp.sum(parts_ref[...].astype(F32), axis=0)
    grad_ref[...] = grad
    new_first = 0.9 * first_ref[...] + 0.1 * grad
    new_second = 0.999 * second_ref[...] + 0.001 * grad * grad
    corrected = new_first / (1.0 - 0.9**STEP)
    scaled = jnp.sqrt(new_second / (1.0 - 0.999**STEP)) + 1e-08
    out_ref[...] = jnp.broadcast_to((corrected / scaled)[None], out_ref.shape).astype(BF16)


def direction_of(parts, first, second, peers):
    return pl.pallas_call(
        direction_kernel,
        in_specs=[whole(), whole(), whole()],
        out_specs=[whole(), whole()],
        out_shape=[
            jax.ShapeDtypeStruct(first.shape, F32),
            jax.ShapeDtypeStruct((peers,) + parts.shape[1:], BF16),
        ],
        compiler_params=pltpu.CompilerParams(vmem_limit_bytes=16 * 1024 * 1024),
    )(parts, first, second)


def expand_mine_kernel(basis_ref, picks_ref, mine_ref, out_ref, ordered_ref):
    _, nx, part, _ = mine_ref.shape
    half = 2 * part
    core = lax.axis_index("c")
    for h in range(2):
        pick = picks_ref[core if h == 0 else 1 - core]
        ordered_ref[:, h * half : (h + 1) * half] = jnp.dot(
            basis_ref[...], pick, preferred_element_type=F32
        ).astype(BF16)
    for i in range(nx):
        rows = jnp.concatenate([mine_ref[0, i], mine_ref[1, i]], axis=0)
        out_ref[i] = jnp.dot(ordered_ref[:, :half], rows, preferred_element_type=F32)


def expand_mine(basis, picks, mine):
    _, nx, part, cols = mine.shape
    rows = basis.shape[0]
    return pl.pallas_call(
        expand_mine_kernel,
        in_specs=[whole(), whole(), whole()],
        out_specs=[whole(), whole()],
        out_shape=[
            jax.ShapeDtypeStruct((nx, rows, cols), F32),
            jax.ShapeDtypeStruct(basis.shape, BF16),
        ],
        compiler_params=pltpu.CompilerParams(vmem_limit_bytes=24 * 1024 * 1024),
        cost_estimate=pl.CostEstimate(
            flops=4 * rows * part * nx * cols, bytes_accessed=4 * nx * rows * cols, transcendentals=0
        ),
    )(basis, picks, mine)


def expand_kernel(tiles, basis_ref, other_ref, mine_ref, out_ref, done, sems):
    _, nx, part, cols = other_ref.shape
    size = basis_ref.shape[0] // tiles
    copies = []
    others = [jnp.concatenate([other_ref[0, i], other_ref[1, i]], axis=0) for i in range(nx)]
    for t in range(tiles):
        rows = pl.ds(t * size, size)
        for i in range(nx):
            acc = mine_ref[i, rows, :] + jnp.dot(
                basis_ref[rows, 2 * part :], others[i], preferred_element_type=F32
            )
            done[rows, pl.ds(i * cols, cols)] = acc.astype(BF16)
        copies.append(pltpu.make_async_copy(done.at[rows], out_ref.at[rows], sems.at[t]))
        copies[-1].start()
    for copy in copies:
        copy.wait()


def expand(basis, other, mine, tiles=5):
    _, nx, _, cols = other.shape
    rows = basis.shape[0]
    return pl.pallas_call(
        functools.partial(expand_kernel, tiles),
        in_specs=[whole(), whole(), whole()],
        out_specs=pl.BlockSpec(memory_space=pl.ANY),
        out_shape=jax.ShapeDtypeStruct((rows, nx * cols), BF16),
        scratch_shapes=[pltpu.VMEM((rows, nx * cols), BF16), pltpu.SemaphoreType.DMA((tiles,))],
        compiler_params=pltpu.CompilerParams(vmem_limit_bytes=24 * 1024 * 1024),
    )(basis, other, mine)


def per_device(ny, nz, nx, inputs, out_grad, basis, moment_first, moment_second):
    rank = basis.shape[1]
    tokens = inputs.shape[0]
    groups = ny * nz
    own, cols = moment_first.shape
    half = rank // 2
    swap = [(0, 1), (1, 0)]

    theirs = lax.ppermute(out_grad, "c", swap)
    picks = rank_order(rank, own, ny, nz)
    partial = project(inputs, basis, picks)
    parts = lax.all_to_all(partial.reshape(nx, tokens // nx, rank), "x", 0, 0)

    sides, theirs = lax.optimization_barrier((combine(parts, picks), theirs))
    rows = lax.all_to_all(sides, ("c", "x"), 0, 0).reshape(2, tokens, half)
    chip = project_grad(rows, out_grad, theirs).reshape(groups, own, cols)
    grad_shard, direction = direction_of(
        lax.all_to_all(chip, ("zl", "y", "zh"), 0, 0), moment_first, moment_second, groups // 2
    )
    gathered = lax.all_to_all(direction, ("y", "zh"), 0, 0).reshape(half // 2, cols)
    mine, grad_shard = lax.optimization_barrier((spread(gathered, ("zl", "x"), 2 * nx), grad_shard))
    mine = mine.reshape(2, nx, half // 2, cols)

    other = lax.ppermute(mine, "c", swap)
    new_first = 0.9 * moment_first + 0.1 * grad_shard
    new_second = 0.999 * moment_second + 0.001 * grad_shard * grad_shard
    done, ordered = expand_mine(basis, picks, mine)
    return (expand(ordered, other, done), new_first, new_second)


def solution(mesh):
    ny, nz, nx = 8, 8, mesh.devices.shape[1]
    split = Mesh(mesh.devices.reshape(ny, nz // 2, 2, 2, nx), ("y", "zh", "zl", "c", "x"))
    dp = ("y", "zh", "zl", "c")

    def body(*args):
        return per_device(ny, nz, nx, *args)

    return jax.shard_map(
        body,
        mesh=split,
        in_specs=(P(dp, "x"), P(dp, "x"), P("x", None), P(dp, "x"), P(dp, "x")),
        out_specs=(P("x", None), P(dp, "x"), P(dp, "x")),
        check_vma=False,
    )
```

```python
import functools

import jax
import jax.numpy as jnp
from jax import lax
from jax.experimental import pallas as pl
from jax.experimental.pallas import tpu as pltpu
from jax.sharding import Mesh, PartitionSpec as P

STEP = 10
F32 = jnp.float32
BF16 = jnp.bfloat16


def spread(block, axes, n):
    return lax.all_to_all(jnp.broadcast_to(block[None], (n,) + block.shape), axes, 0, 0)


def whole():
    return pl.BlockSpec(memory_space=pltpu.VMEM)


def order_kernel(own, ny, nz, out_ref):
    _, rank, half = out_ref.shape
    old = lax.broadcasted_iota(jnp.int32, (rank, half), 0)
    new = lax.broadcasted_iota(jnp.int32, (rank, half), 1)
    block = new // own
    pair = block % (nz // 2)
    y = block // (nz // 2) % ny
    parity = block // (nz // 2 * ny)
    first = ((y * nz + pair * 2 + parity) * 2) * own + new % own
    for c in range(2):
        out_ref[c] = (old == first + c * own).astype(F32).astype(BF16)


def rank_order(rank, own, ny, nz):
    return pl.pallas_call(
        functools.partial(order_kernel, own, ny, nz),
        in_specs=[],
        out_specs=whole(),
        out_shape=jax.ShapeDtypeStruct((2, rank, rank // 2), BF16),
        compiler_params=pltpu.CompilerParams(vmem_limit_bytes=16 * 1024 * 1024),
        cost_estimate=pl.CostEstimate(flops=4 * 10**9, bytes_accessed=8 * 10**6, transcendentals=0),
    )()


def project_kernel(inputs_ref, basis_ref, picks_ref, out_ref):
    del picks_ref
    out_ref[...] = jnp.dot(inputs_ref[...], basis_ref[...], preferred_element_type=F32).astype(BF16)


def project(inputs, basis, picks):
    return pl.pallas_call(
        project_kernel,
        in_specs=[whole(), whole(), whole()],
        out_specs=whole(),
        out_shape=jax.ShapeDtypeStruct((inputs.shape[0], basis.shape[1]), BF16),
        compiler_params=pltpu.CompilerParams(vmem_limit_bytes=16 * 1024 * 1024),
    )(inputs, basis, picks)


def combine_kernel(parts_ref, picks_ref, out_ref):
    nx = parts_ref.shape[0]
    total = parts_ref[0].astype(F32)
    for i in range(1, nx):
        total += parts_ref[i].astype(F32)
    total = total.astype(BF16)
    for c in range(2):
        side = jnp.dot(total, picks_ref[c], preferred_element_type=F32).astype(BF16)
        for i in range(nx):
            out_ref[2 * i + c] = side


def combine(parts, picks):
    nx, tokens, rank = parts.shape
    return pl.pallas_call(
        combine_kernel,
        in_specs=[whole(), whole()],
        out_specs=whole(),
        out_shape=jax.ShapeDtypeStruct((2 * nx, tokens, rank // 2), BF16),
        compiler_params=pltpu.CompilerParams(vmem_limit_bytes=16 * 1024 * 1024),
    )(parts, picks)


def project_grad_kernel(rows_ref, own_ref, theirs_ref, out_ref):
    core = lax.axis_index("c")
    nx = rows_ref.shape[0]
    mine = jnp.concatenate([rows_ref[i, core] for i in range(nx)], axis=0)
    others = jnp.concatenate([rows_ref[i, 1 - core] for i in range(nx)], axis=0)
    total = lax.dot_general(
        mine, own_ref[...], (((0,), (0,)), ((), ())), preferred_element_type=F32
    )
    total += lax.dot_general(
        others, theirs_ref[...], (((0,), (0,)), ((), ())), preferred_element_type=F32
    )
    out_ref[...] = total.astype(BF16)


def project_grad(rows, own, theirs):
    return pl.pallas_call(
        project_grad_kernel,
        in_specs=[whole(), whole(), whole()],
        out_specs=whole(),
        out_shape=jax.ShapeDtypeStruct((rows.shape[3], own.shape[1]), BF16),
        compiler_params=pltpu.CompilerParams(vmem_limit_bytes=16 * 1024 * 1024),
    )(rows, own, theirs)


def direction_kernel(parts_ref, first_ref, second_ref, grad_ref, out_ref):
    grad = jnp.sum(parts_ref[...].astype(F32), axis=0)
    grad_ref[...] = grad
    new_first = 0.9 * first_ref[...] + 0.1 * grad
    new_second = 0.999 * second_ref[...] + 0.001 * grad * grad
    corrected = new_first / (1.0 - 0.9**STEP)
    scaled = jnp.sqrt(new_second / (1.0 - 0.999**STEP)) + 1e-08
    out_ref[...] = jnp.broadcast_to((corrected / scaled)[None], out_ref.shape).astype(BF16)


def direction_of(parts, first, second, peers):
    return pl.pallas_call(
        direction_kernel,
        in_specs=[whole(), whole(), whole()],
        out_specs=[whole(), whole()],
        out_shape=[
            jax.ShapeDtypeStruct(first.shape, F32),
            jax.ShapeDtypeStruct((peers,) + parts.shape[1:], BF16),
        ],
        compiler_params=pltpu.CompilerParams(vmem_limit_bytes=16 * 1024 * 1024),
    )(parts, first, second)


def expand_mine_kernel(basis_ref, picks_ref, mine_ref, out_ref, ordered_ref):
    nx, half, _ = mine_ref.shape
    core = lax.axis_index("c")
    for h in range(2):
        pick = picks_ref[core if h == 0 else 1 - core]
        ordered_ref[:, h * half : (h + 1) * half] = jnp.dot(
            basis_ref[...], pick, preferred_element_type=F32
        ).astype(BF16)
    for i in range(nx):
        out_ref[i] = jnp.dot(ordered_ref[:, :half], mine_ref[i], preferred_element_type=F32)


def expand_mine(basis, picks, mine):
    nx, half, cols = mine.shape
    rows = basis.shape[0]
    return pl.pallas_call(
        expand_mine_kernel,
        in_specs=[whole(), whole(), whole()],
        out_specs=[whole(), whole()],
        out_shape=[
            jax.ShapeDtypeStruct((nx, rows, cols), F32),
            jax.ShapeDtypeStruct(basis.shape, BF16),
        ],
        compiler_params=pltpu.CompilerParams(vmem_limit_bytes=24 * 1024 * 1024),
        cost_estimate=pl.CostEstimate(
            flops=2 * rows * half * nx * cols, bytes_accessed=4 * nx * rows * cols, transcendentals=0
        ),
    )(basis, picks, mine)


def expand_kernel(tiles, basis_ref, other_ref, mine_ref, out_ref, done, sems):
    nx, half, cols = other_ref.shape
    size = basis_ref.shape[0] // tiles
    copies = []
    for t in range(tiles):
        rows = pl.ds(t * size, size)
        for i in range(nx):
            acc = mine_ref[i, rows, :] + jnp.dot(
                basis_ref[rows, half:], other_ref[i], preferred_element_type=F32
            )
            done[rows, pl.ds(i * cols, cols)] = acc.astype(BF16)
        copies.append(pltpu.make_async_copy(done.at[rows], out_ref.at[rows], sems.at[t]))
        copies[-1].start()
    for copy in copies:
        copy.wait()


def expand(basis, other, mine, tiles=5):
    nx, _, cols = other.shape
    rows = basis.shape[0]
    return pl.pallas_call(
        functools.partial(expand_kernel, tiles),
        in_specs=[whole(), whole(), whole()],
        out_specs=pl.BlockSpec(memory_space=pl.ANY),
        out_shape=jax.ShapeDtypeStruct((rows, nx * cols), BF16),
        scratch_shapes=[pltpu.VMEM((rows, nx * cols), BF16), pltpu.SemaphoreType.DMA((tiles,))],
        compiler_params=pltpu.CompilerParams(vmem_limit_bytes=24 * 1024 * 1024),
    )(basis, other, mine)


def per_device(ny, nz, nx, inputs, out_grad, basis, moment_first, moment_second):
    rank = basis.shape[1]
    tokens = inputs.shape[0]
    groups = ny * nz
    own, cols = moment_first.shape
    half = rank // 2
    swap = [(0, 1), (1, 0)]

    theirs = lax.ppermute(out_grad, "c", swap)
    picks = rank_order(rank, own, ny, nz)
    partial = project(inputs, basis, picks)
    parts = lax.all_to_all(partial.reshape(nx, tokens // nx, rank), "x", 0, 0)

    sides, theirs = lax.optimization_barrier((combine(parts, picks), theirs))
    rows = lax.all_to_all(sides, ("x", "c"), 0, 0).reshape(nx, 2, tokens // nx, half)
    chip = project_grad(rows, out_grad, theirs).reshape(groups, own, cols)
    grad_shard, direction = direction_of(
        lax.all_to_all(chip, ("zl", "y", "zh"), 0, 0), moment_first, moment_second, groups // 2
    )
    gathered = lax.all_to_all(direction, ("y", "zh"), 0, 0).reshape(half // 2, cols)
    mine, grad_shard = lax.optimization_barrier((spread(gathered, ("x", "zl"), 2 * nx), grad_shard))
    mine = mine.reshape(nx, half, cols)

    other = lax.ppermute(mine, "c", swap)
    new_first = 0.9 * moment_first + 0.1 * grad_shard
    new_second = 0.999 * moment_second + 0.001 * grad_shard * grad_shard
    done, ordered = expand_mine(basis, picks, mine)
    return (expand(ordered, other, done), new_first, new_second)


def solution(mesh):
    ny, nz, nx = 8, 8, mesh.devices.shape[1]
    split = Mesh(mesh.devices.reshape(ny, nz // 2, 2, 2, nx), ("y", "zh", "zl", "c", "x"))
    dp = ("y", "zh", "zl", "c")

    def body(*args):
        return per_device(ny, nz, nx, *args)

    return jax.shard_map(
        body,
        mesh=split,
        in_specs=(P(dp, "x"), P(dp, "x"), P("x", None), P(dp, "x"), P(dp, "x")),
        out_specs=(P("x", None), P(dp, "x"), P(dp, "x")),
        check_vma=False,
    )
```

```python
import functools

import jax
import jax.numpy as jnp
from jax import lax
from jax.experimental import pallas as pl
from jax.experimental.pallas import tpu as pltpu
from jax.sharding import Mesh, PartitionSpec as P

STEP = 10
F32 = jnp.float32
BF16 = jnp.bfloat16


def spread(block, axes, n):
    return lax.all_to_all(jnp.broadcast_to(block[None], (n,) + block.shape), axes, 0, 0)


def whole():
    return pl.BlockSpec(memory_space=pltpu.VMEM)


def order_kernel(own, ny, nz, out_ref):
    _, rank, half = out_ref.shape
    old = lax.broadcasted_iota(jnp.int32, (rank, half), 0)
    new = lax.broadcasted_iota(jnp.int32, (rank, half), 1)
    block = new // own
    pair = block % (nz // 2)
    y = block // (nz // 2) % ny
    parity = block // (nz // 2 * ny)
    first = ((y * nz + pair * 2 + parity) * 2) * own + new % own
    for c in range(2):
        out_ref[c] = (old == first + c * own).astype(F32).astype(BF16)


def rank_order(rank, own, ny, nz):
    return pl.pallas_call(
        functools.partial(order_kernel, own, ny, nz),
        in_specs=[],
        out_specs=whole(),
        out_shape=jax.ShapeDtypeStruct((2, rank, rank // 2), BF16),
        compiler_params=pltpu.CompilerParams(vmem_limit_bytes=16 * 1024 * 1024),
        cost_estimate=pl.CostEstimate(flops=4 * 10**9, bytes_accessed=8 * 10**6, transcendentals=0),
    )()


def project_kernel(inputs_ref, basis_ref, picks_ref, out_ref):
    size = out_ref.shape[1]
    part = jnp.dot(inputs_ref[...], basis_ref[...], preferred_element_type=F32).astype(BF16)
    for c in range(2):
        side = jnp.dot(part, picks_ref[c], preferred_element_type=F32).astype(BF16)
        for i in range(out_ref.shape[0] // 2):
            out_ref[2 * i + c] = side[i * size : (i + 1) * size]


def project(inputs, basis, picks, nx):
    tokens = inputs.shape[0]
    return pl.pallas_call(
        project_kernel,
        in_specs=[whole(), whole(), whole()],
        out_specs=whole(),
        out_shape=jax.ShapeDtypeStruct((2 * nx, tokens // nx, picks.shape[2]), BF16),
        compiler_params=pltpu.CompilerParams(vmem_limit_bytes=16 * 1024 * 1024),
    )(inputs, basis, picks)


def combine_kernel(parts_ref, out_ref):
    nx = out_ref.shape[0]
    for c in range(2):
        total = parts_ref[c].astype(F32)
        for i in range(1, nx):
            total += parts_ref[2 * i + c].astype(F32)
        total = total.astype(BF16)
        for i in range(nx):
            out_ref[i, c] = total


def combine(parts):
    both, tokens, half = parts.shape
    return pl.pallas_call(
        combine_kernel,
        in_specs=[whole()],
        out_specs=whole(),
        out_shape=jax.ShapeDtypeStruct((both // 2, 2, tokens, half), BF16),
        compiler_params=pltpu.CompilerParams(vmem_limit_bytes=16 * 1024 * 1024),
    )(parts)


def project_grad_kernel(rows_ref, own_ref, theirs_ref, out_ref):
    core = lax.axis_index("c")
    nx = rows_ref.shape[0]
    mine = jnp.concatenate([rows_ref[i, core] for i in range(nx)], axis=0)
    others = jnp.concatenate([rows_ref[i, 1 - core] for i in range(nx)], axis=0)
    total = lax.dot_general(
        mine, own_ref[...], (((0,), (0,)), ((), ())), preferred_element_type=F32
    )
    total += lax.dot_general(
        others, theirs_ref[...], (((0,), (0,)), ((), ())), preferred_element_type=F32
    )
    out_ref[...] = total.astype(BF16)


def project_grad(rows, own, theirs):
    return pl.pallas_call(
        project_grad_kernel,
        in_specs=[whole(), whole(), whole()],
        out_specs=whole(),
        out_shape=jax.ShapeDtypeStruct((rows.shape[3], own.shape[1]), BF16),
        compiler_params=pltpu.CompilerParams(vmem_limit_bytes=16 * 1024 * 1024),
    )(rows, own, theirs)


def direction_kernel(parts_ref, first_ref, second_ref, grad_ref, out_ref):
    grad = jnp.sum(parts_ref[...].astype(F32), axis=0)
    grad_ref[...] = grad
    new_first = 0.9 * first_ref[...] + 0.1 * grad
    new_second = 0.999 * second_ref[...] + 0.001 * grad * grad
    corrected = new_first / (1.0 - 0.9**STEP)
    scaled = jnp.sqrt(new_second / (1.0 - 0.999**STEP)) + 1e-08
    out_ref[...] = jnp.broadcast_to((corrected / scaled)[None], out_ref.shape).astype(BF16)


def direction_of(parts, first, second, peers):
    return pl.pallas_call(
        direction_kernel,
        in_specs=[whole(), whole(), whole()],
        out_specs=[whole(), whole()],
        out_shape=[
            jax.ShapeDtypeStruct(first.shape, F32),
            jax.ShapeDtypeStruct((peers,) + parts.shape[1:], BF16),
        ],
        compiler_params=pltpu.CompilerParams(vmem_limit_bytes=16 * 1024 * 1024),
    )(parts, first, second)


def expand_mine_kernel(basis_ref, picks_ref, mine_ref, out_ref, ordered_ref):
    nx, half, _ = mine_ref.shape
    core = lax.axis_index("c")
    for h in range(2):
        pick = picks_ref[core if h == 0 else 1 - core]
        ordered_ref[:, h * half : (h + 1) * half] = jnp.dot(
            basis_ref[...], pick, preferred_element_type=F32
        ).astype(BF16)
    for i in range(nx):
        out_ref[i] = jnp.dot(ordered_ref[:, :half], mine_ref[i], preferred_element_type=F32)


def expand_mine(basis, picks, mine):
    nx, half, cols = mine.shape
    rows = basis.shape[0]
    return pl.pallas_call(
        expand_mine_kernel,
        in_specs=[whole(), whole(), whole()],
        out_specs=[whole(), whole()],
        out_shape=[
            jax.ShapeDtypeStruct((nx, rows, cols), F32),
            jax.ShapeDtypeStruct(basis.shape, BF16),
        ],
        compiler_params=pltpu.CompilerParams(vmem_limit_bytes=24 * 1024 * 1024),
        cost_estimate=pl.CostEstimate(
            flops=2 * rows * half * nx * cols, bytes_accessed=4 * nx * rows * cols, transcendentals=0
        ),
    )(basis, picks, mine)


def expand_kernel(tiles, basis_ref, other_ref, mine_ref, out_ref, done, sems):
    nx, half, cols = other_ref.shape
    size = basis_ref.shape[0] // tiles
    copies = []
    for t in range(tiles):
        rows = pl.ds(t * size, size)
        for i in range(nx):
            acc = mine_ref[i, rows, :] + jnp.dot(
                basis_ref[rows, half:], other_ref[i], preferred_element_type=F32
            )
            done[rows, pl.ds(i * cols, cols)] = acc.astype(BF16)
        copies.append(pltpu.make_async_copy(done.at[rows], out_ref.at[rows], sems.at[t]))
        copies[-1].start()
    for copy in copies:
        copy.wait()


def expand(basis, other, mine, tiles=5):
    nx, _, cols = other.shape
    rows = basis.shape[0]
    return pl.pallas_call(
        functools.partial(expand_kernel, tiles),
        in_specs=[whole(), whole(), whole()],
        out_specs=pl.BlockSpec(memory_space=pl.ANY),
        out_shape=jax.ShapeDtypeStruct((rows, nx * cols), BF16),
        scratch_shapes=[pltpu.VMEM((rows, nx * cols), BF16), pltpu.SemaphoreType.DMA((tiles,))],
        compiler_params=pltpu.CompilerParams(vmem_limit_bytes=24 * 1024 * 1024),
    )(basis, other, mine)


def per_device(ny, nz, nx, inputs, out_grad, basis, moment_first, moment_second):
    rank = basis.shape[1]
    tokens = inputs.shape[0]
    groups = ny * nz
    own, cols = moment_first.shape
    half = rank // 2
    swap = [(0, 1), (1, 0)]

    theirs = lax.ppermute(out_grad, "c", swap)
    picks = rank_order(rank, own, ny, nz)
    parts = lax.all_to_all(project(inputs, basis, picks, nx), ("x", "c"), 0, 0)
    sums, theirs = lax.optimization_barrier((combine(parts), theirs))
    rows = lax.all_to_all(sums, "x", 0, 0)
    chip = project_grad(rows, out_grad, theirs).reshape(groups, own, cols)
    grad_shard, direction = direction_of(
        lax.all_to_all(chip, ("zl", "y", "zh"), 0, 0), moment_first, moment_second, groups // 2
    )
    gathered = lax.all_to_all(direction, ("y", "zh"), 0, 0).reshape(half // 2, cols)
    mine, grad_shard = lax.optimization_barrier((spread(gathered, ("x", "zl"), 2 * nx), grad_shard))
    mine = mine.reshape(nx, half, cols)

    other = lax.ppermute(mine, "c", swap)
    new_first = 0.9 * moment_first + 0.1 * grad_shard
    new_second = 0.999 * moment_second + 0.001 * grad_shard * grad_shard
    done, ordered = expand_mine(basis, picks, mine)
    return (expand(ordered, other, done), new_first, new_second)


def solution(mesh):
    ny, nz, nx = 8, 8, mesh.devices.shape[1]
    split = Mesh(mesh.devices.reshape(ny, nz // 2, 2, 2, nx), ("y", "zh", "zl", "c", "x"))
    dp = ("y", "zh", "zl", "c")

    def body(*args):
        return per_device(ny, nz, nx, *args)

    return jax.shard_map(
        body,
        mesh=split,
        in_specs=(P(dp, "x"), P(dp, "x"), P("x", None), P(dp, "x"), P(dp, "x")),
        out_specs=(P("x", None), P(dp, "x"), P(dp, "x")),
        check_vma=False,
    )
```

```python
import functools

import jax
import jax.numpy as jnp
from jax import lax
from jax.experimental import pallas as pl
from jax.experimental.pallas import tpu as pltpu
from jax.sharding import Mesh, PartitionSpec as P

STEP = 10
MIRRORED = 1
F32 = jnp.float32
BF16 = jnp.bfloat16
PLANE = ("y", "zh", "zl", "c")


def spread(block, axes, n):
    return lax.all_to_all(jnp.broadcast_to(block[None], (n,) + block.shape), axes, 0, 0)


def whole():
    return pl.BlockSpec(memory_space=pltpu.VMEM)


def order_kernel(own, ny, nz, out_ref):
    _, rank, half = out_ref.shape
    old = lax.broadcasted_iota(jnp.int32, (rank, half), 0)
    new = lax.broadcasted_iota(jnp.int32, (rank, half), 1)
    block = new // own
    pair = block % (nz // 2)
    y = block // (nz // 2) % ny
    parity = block // (nz // 2 * ny)
    first = ((y * nz + pair * 2 + parity) * 2) * own + new % own
    mirrored = (((ny - 1 - y) * nz + (nz // 2 - 1 - pair) * 2 + parity) * 2) * own + new % own
    for c in range(2):
        start = mirrored if c == MIRRORED else first
        out_ref[c] = (old == start + c * own).astype(F32).astype(BF16)


def plane_groups(ny, nz, parities):
    pairs = nz // 2
    groups = []
    for some in parities:
        for c in range(2):
            order = [(p, y, z) for p in some for y in range(ny) for z in range(pairs)]
            if c == MIRRORED:
                order = [(p, ny - 1 - y, pairs - 1 - z) for p, y, z in order]
            groups.append([((y * pairs + z) * 2 + p) * 2 + c for p, y, z in order])
    return groups


def rank_order(rank, own, ny, nz):
    return pl.pallas_call(
        functools.partial(order_kernel, own, ny, nz),
        in_specs=[],
        out_specs=whole(),
        out_shape=jax.ShapeDtypeStruct((2, rank, rank // 2), BF16),
        compiler_params=pltpu.CompilerParams(vmem_limit_bytes=16 * 1024 * 1024),
        cost_estimate=pl.CostEstimate(flops=4 * 10**9, bytes_accessed=8 * 10**6, transcendentals=0),
    )()


def project_kernel(inputs_ref, basis_ref, picks_ref, out_ref):
    size = out_ref.shape[1]
    part = jnp.dot(inputs_ref[...], basis_ref[...], preferred_element_type=F32).astype(BF16)
    for c in range(2):
        side = jnp.dot(part, picks_ref[c], preferred_element_type=F32).astype(BF16)
        for i in range(out_ref.shape[0] // 2):
            out_ref[2 * i + c] = side[i * size : (i + 1) * size]


def project(inputs, basis, picks, nx):
    tokens = inputs.shape[0]
    return pl.pallas_call(
        project_kernel,
        in_specs=[whole(), whole(), whole()],
        out_specs=whole(),
        out_shape=jax.ShapeDtypeStruct((2 * nx, tokens // nx, picks.shape[2]), BF16),
        compiler_params=pltpu.CompilerParams(vmem_limit_bytes=16 * 1024 * 1024),
    )(inputs, basis, picks)


def combine_kernel(parts_ref, out_ref):
    nx = out_ref.shape[0]
    for c in range(2):
        total = parts_ref[c].astype(F32)
        for i in range(1, nx):
            total += parts_ref[2 * i + c].astype(F32)
        total = total.astype(BF16)
        for i in range(nx):
            out_ref[i, c] = total


def combine(parts):
    both, tokens, half = parts.shape
    return pl.pallas_call(
        combine_kernel,
        in_specs=[whole()],
        out_specs=whole(),
        out_shape=jax.ShapeDtypeStruct((both // 2, 2, tokens, half), BF16),
        compiler_params=pltpu.CompilerParams(vmem_limit_bytes=16 * 1024 * 1024),
    )(parts)


def project_grad_kernel(rows_ref, own_ref, theirs_ref, out_ref):
    core = lax.axis_index("c")
    nx = rows_ref.shape[0]
    mine = jnp.concatenate([rows_ref[i, core] for i in range(nx)], axis=0)
    others = jnp.concatenate([rows_ref[i, 1 - core] for i in range(nx)], axis=0)
    total = lax.dot_general(
        mine, own_ref[...], (((0,), (0,)), ((), ())), preferred_element_type=F32
    )
    total += lax.dot_general(
        others, theirs_ref[...], (((0,), (0,)), ((), ())), preferred_element_type=F32
    )
    out_ref[...] = total.astype(BF16)


def project_grad(rows, own, theirs):
    return pl.pallas_call(
        project_grad_kernel,
        in_specs=[whole(), whole(), whole()],
        out_specs=whole(),
        out_shape=jax.ShapeDtypeStruct((rows.shape[3], own.shape[1]), BF16),
        compiler_params=pltpu.CompilerParams(vmem_limit_bytes=16 * 1024 * 1024),
    )(rows, own, theirs)


def direction_kernel(parts_ref, first_ref, second_ref, grad_ref, out_ref):
    grad = jnp.sum(parts_ref[...].astype(F32), axis=0)
    grad_ref[...] = grad
    new_first = 0.9 * first_ref[...] + 0.1 * grad
    new_second = 0.999 * second_ref[...] + 0.001 * grad * grad
    corrected = new_first / (1.0 - 0.9**STEP)
    scaled = jnp.sqrt(new_second / (1.0 - 0.999**STEP)) + 1e-08
    out_ref[...] = jnp.broadcast_to((corrected / scaled)[None], out_ref.shape).astype(BF16)


def direction_of(parts, first, second, peers):
    return pl.pallas_call(
        direction_kernel,
        in_specs=[whole(), whole(), whole()],
        out_specs=[whole(), whole()],
        out_shape=[
            jax.ShapeDtypeStruct(first.shape, F32),
            jax.ShapeDtypeStruct((peers,) + parts.shape[1:], BF16),
        ],
        compiler_params=pltpu.CompilerParams(vmem_limit_bytes=16 * 1024 * 1024),
    )(parts, first, second)


def expand_mine_kernel(basis_ref, picks_ref, mine_ref, out_ref, ordered_ref):
    nx, half, _ = mine_ref.shape
    core = lax.axis_index("c")
    for h in range(2):
        pick = picks_ref[core if h == 0 else 1 - core]
        ordered_ref[:, h * half : (h + 1) * half] = jnp.dot(
            basis_ref[...], pick, preferred_element_type=F32
        ).astype(BF16)
    for i in range(nx):
        out_ref[i] = jnp.dot(ordered_ref[:, :half], mine_ref[i], preferred_element_type=F32)


def expand_mine(basis, picks, mine):
    nx, half, cols = mine.shape
    rows = basis.shape[0]
    return pl.pallas_call(
        expand_mine_kernel,
        in_specs=[whole(), whole(), whole()],
        out_specs=[whole(), whole()],
        out_shape=[
            jax.ShapeDtypeStruct((nx, rows, cols), F32),
            jax.ShapeDtypeStruct(basis.shape, BF16),
        ],
        compiler_params=pltpu.CompilerParams(vmem_limit_bytes=24 * 1024 * 1024),
        cost_estimate=pl.CostEstimate(
            flops=2 * rows * half * nx * cols, bytes_accessed=4 * nx * rows * cols, transcendentals=0
        ),
    )(basis, picks, mine)


def expand_kernel(tiles, basis_ref, other_ref, mine_ref, out_ref, done, sems):
    nx, half, cols = other_ref.shape
    size = basis_ref.shape[0] // tiles
    copies = []
    for t in range(tiles):
        rows = pl.ds(t * size, size)
        for i in range(nx):
            acc = mine_ref[i, rows, :] + jnp.dot(
                basis_ref[rows, half:], other_ref[i], preferred_element_type=F32
            )
            done[rows, pl.ds(i * cols, cols)] = acc.astype(BF16)
        copies.append(pltpu.make_async_copy(done.at[rows], out_ref.at[rows], sems.at[t]))
        copies[-1].start()
    for copy in copies:
        copy.wait()


def expand(basis, other, mine, tiles=5):
    nx, _, cols = other.shape
    rows = basis.shape[0]
    return pl.pallas_call(
        functools.partial(expand_kernel, tiles),
        in_specs=[whole(), whole(), whole()],
        out_specs=pl.BlockSpec(memory_space=pl.ANY),
        out_shape=jax.ShapeDtypeStruct((rows, nx * cols), BF16),
        scratch_shapes=[pltpu.VMEM((rows, nx * cols), BF16), pltpu.SemaphoreType.DMA((tiles,))],
        compiler_params=pltpu.CompilerParams(vmem_limit_bytes=24 * 1024 * 1024),
    )(basis, other, mine)


def per_device(ny, nz, nx, inputs, out_grad, basis, moment_first, moment_second):
    rank = basis.shape[1]
    tokens = inputs.shape[0]
    groups = ny * nz
    own, cols = moment_first.shape
    half = rank // 2
    swap = [(0, 1), (1, 0)]

    theirs = lax.ppermute(out_grad, "c", swap)
    picks = rank_order(rank, own, ny, nz)
    parts = lax.all_to_all(project(inputs, basis, picks, nx), ("x", "c"), 0, 0)
    sums, theirs = lax.optimization_barrier((combine(parts), theirs))
    rows = lax.all_to_all(sums, "x", 0, 0)
    chip = project_grad(rows, out_grad, theirs).reshape(groups, own, cols)
    grad_shard, direction = direction_of(
        lax.all_to_all(chip, PLANE, 0, 0, axis_index_groups=plane_groups(ny, nz, [(0, 1)])), moment_first, moment_second, groups // 2
    )
    gathered = lax.all_to_all(
        direction, PLANE, 0, 0, axis_index_groups=plane_groups(ny, nz, [(0,), (1,)])
    ).reshape(half // 2, cols)
    mine, grad_shard = lax.optimization_barrier((spread(gathered, ("x", "zl"), 2 * nx), grad_shard))
    mine = mine.reshape(nx, half, cols)

    other = lax.ppermute(mine, "c", swap)
    new_first = 0.9 * moment_first + 0.1 * grad_shard
    new_second = 0.999 * moment_second + 0.001 * grad_shard * grad_shard
    done, ordered = expand_mine(basis, picks, mine)
    return (expand(ordered, other, done), new_first, new_second)


def solution(mesh):
    ny, nz, nx = 8, 8, mesh.devices.shape[1]
    split = Mesh(mesh.devices.reshape(ny, nz // 2, 2, 2, nx), ("y", "zh", "zl", "c", "x"))
    dp = ("y", "zh", "zl", "c")

    def body(*args):
        return per_device(ny, nz, nx, *args)

    return jax.shard_map(
        body,
        mesh=split,
        in_specs=(P(dp, "x"), P(dp, "x"), P("x", None), P(dp, "x"), P(dp, "x")),
        out_specs=(P("x", None), P(dp, "x"), P(dp, "x")),
        check_vma=False,
    )
```

```python
import functools

import jax
import jax.numpy as jnp
from jax import lax
from jax.experimental import pallas as pl
from jax.experimental.pallas import tpu as pltpu
from jax.sharding import Mesh, PartitionSpec as P

STEP = 10
MIRRORED = 1
F32 = jnp.float32
BF16 = jnp.bfloat16
PLANE = ("y", "zh", "zl", "c")


def spread(block, axes, n):
    return lax.all_to_all(jnp.broadcast_to(block[None], (n,) + block.shape), axes, 0, 0)


def whole():
    return pl.BlockSpec(memory_space=pltpu.VMEM)


def order_kernel(own, ny, nz, out_ref):
    _, rank, half = out_ref.shape
    old = lax.broadcasted_iota(jnp.int32, (rank, half), 0)
    new = lax.broadcasted_iota(jnp.int32, (rank, half), 1)
    block = new // own
    pair = block % (nz // 2)
    y = block // (nz // 2) % ny
    parity = block // (nz // 2 * ny)
    first = ((y * nz + pair * 2 + parity) * 2) * own + new % own
    mirrored = (((ny - 1 - y) * nz + (nz // 2 - 1 - pair) * 2 + parity) * 2) * own + new % own
    for n, (start, c) in enumerate([(first, 0), (mirrored, 1), (first, 1)]):
        out_ref[n] = (old == start + c * own).astype(F32).astype(BF16)


def plane_groups(ny, nz, parities):
    pairs = nz // 2
    groups = []
    for some in parities:
        for c in range(2):
            order = [(p, y, z) for p in some for y in range(ny) for z in range(pairs)]
            if c == MIRRORED:
                order = [(p, ny - 1 - y, pairs - 1 - z) for p, y, z in order]
            groups.append([((y * pairs + z) * 2 + p) * 2 + c for p, y, z in order])
    return groups


def rank_order(rank, own, ny, nz):
    return pl.pallas_call(
        functools.partial(order_kernel, own, ny, nz),
        in_specs=[],
        out_specs=whole(),
        out_shape=jax.ShapeDtypeStruct((3, rank, rank // 2), BF16),
        compiler_params=pltpu.CompilerParams(vmem_limit_bytes=16 * 1024 * 1024),
        cost_estimate=pl.CostEstimate(flops=4 * 10**9, bytes_accessed=8 * 10**6, transcendentals=0),
    )()


def project_kernel(inputs_ref, basis_ref, picks_ref, out_ref):
    size = out_ref.shape[1]
    part = jnp.dot(inputs_ref[...], basis_ref[...], preferred_element_type=F32).astype(BF16)
    for c in range(2):
        side = jnp.dot(part, picks_ref[c], preferred_element_type=F32).astype(BF16)
        for i in range(out_ref.shape[0] // 2):
            out_ref[2 * i + c] = side[i * size : (i + 1) * size]


def project(inputs, basis, picks, nx):
    tokens = inputs.shape[0]
    return pl.pallas_call(
        project_kernel,
        in_specs=[whole(), whole(), whole()],
        out_specs=whole(),
        out_shape=jax.ShapeDtypeStruct((2 * nx, tokens // nx, picks.shape[2]), BF16),
        compiler_params=pltpu.CompilerParams(vmem_limit_bytes=16 * 1024 * 1024),
    )(inputs, basis, picks)


def combine_kernel(parts_ref, out_ref):
    nx = out_ref.shape[0]
    for c in range(2):
        total = parts_ref[c].astype(F32)
        for i in range(1, nx):
            total += parts_ref[2 * i + c].astype(F32)
        total = total.astype(BF16)
        for i in range(nx):
            out_ref[i, c] = total


def combine(parts):
    both, tokens, half = parts.shape
    return pl.pallas_call(
        combine_kernel,
        in_specs=[whole()],
        out_specs=whole(),
        out_shape=jax.ShapeDtypeStruct((both // 2, 2, tokens, half), BF16),
        compiler_params=pltpu.CompilerParams(vmem_limit_bytes=16 * 1024 * 1024),
    )(parts)


def project_grad_kernel(rows_ref, own_ref, theirs_ref, out_ref):
    core = lax.axis_index("c")
    nx = rows_ref.shape[0]
    mine = jnp.concatenate([rows_ref[i, core] for i in range(nx)], axis=0)
    others = jnp.concatenate([rows_ref[i, 1 - core] for i in range(nx)], axis=0)
    total = lax.dot_general(
        mine, own_ref[...], (((0,), (0,)), ((), ())), preferred_element_type=F32
    )
    total += lax.dot_general(
        others, theirs_ref[...], (((0,), (0,)), ((), ())), preferred_element_type=F32
    )
    out_ref[...] = total.astype(BF16)


def project_grad(rows, own, theirs):
    return pl.pallas_call(
        project_grad_kernel,
        in_specs=[whole(), whole(), whole()],
        out_specs=whole(),
        out_shape=jax.ShapeDtypeStruct((rows.shape[3], own.shape[1]), BF16),
        compiler_params=pltpu.CompilerParams(vmem_limit_bytes=16 * 1024 * 1024),
    )(rows, own, theirs)


def direction_kernel(parts_ref, first_ref, second_ref, grad_ref, out_ref):
    grad = jnp.sum(parts_ref[...].astype(F32), axis=0)
    grad_ref[...] = grad
    new_first = 0.9 * first_ref[...] + 0.1 * grad
    new_second = 0.999 * second_ref[...] + 0.001 * grad * grad
    corrected = new_first / (1.0 - 0.9**STEP)
    scaled = jnp.sqrt(new_second / (1.0 - 0.999**STEP)) + 1e-08
    out_ref[...] = jnp.broadcast_to((corrected / scaled)[None], out_ref.shape).astype(BF16)


def direction_of(parts, first, second, peers):
    return pl.pallas_call(
        direction_kernel,
        in_specs=[whole(), whole(), whole()],
        out_specs=[whole(), whole()],
        out_shape=[
            jax.ShapeDtypeStruct(first.shape, F32),
            jax.ShapeDtypeStruct((peers,) + parts.shape[1:], BF16),
        ],
        compiler_params=pltpu.CompilerParams(vmem_limit_bytes=16 * 1024 * 1024),
    )(parts, first, second)


def expand_mine_kernel(basis_ref, picks_ref, mine_ref, out_ref, ordered_ref):
    nx, half, _ = mine_ref.shape
    core = lax.axis_index("c")
    for h in range(2):
        pick = picks_ref[2 * (core if h == 0 else 1 - core)]
        ordered_ref[:, h * half : (h + 1) * half] = jnp.dot(
            basis_ref[...], pick, preferred_element_type=F32
        ).astype(BF16)
    for i in range(nx):
        out_ref[i] = jnp.dot(ordered_ref[:, :half], mine_ref[i], preferred_element_type=F32)


def expand_mine(basis, picks, mine):
    nx, half, cols = mine.shape
    rows = basis.shape[0]
    return pl.pallas_call(
        expand_mine_kernel,
        in_specs=[whole(), whole(), whole()],
        out_specs=[whole(), whole()],
        out_shape=[
            jax.ShapeDtypeStruct((nx, rows, cols), F32),
            jax.ShapeDtypeStruct(basis.shape, BF16),
        ],
        compiler_params=pltpu.CompilerParams(vmem_limit_bytes=24 * 1024 * 1024),
        cost_estimate=pl.CostEstimate(
            flops=2 * rows * half * nx * cols, bytes_accessed=4 * nx * rows * cols, transcendentals=0
        ),
    )(basis, picks, mine)


def expand_kernel(tiles, basis_ref, other_ref, mine_ref, out_ref, done, sems):
    nx, half, cols = other_ref.shape
    size = basis_ref.shape[0] // tiles
    copies = []
    for t in range(tiles):
        rows = pl.ds(t * size, size)
        for i in range(nx):
            acc = mine_ref[i, rows, :] + jnp.dot(
                basis_ref[rows, half:], other_ref[i], preferred_element_type=F32
            )
            done[rows, pl.ds(i * cols, cols)] = acc.astype(BF16)
        copies.append(pltpu.make_async_copy(done.at[rows], out_ref.at[rows], sems.at[t]))
        copies[-1].start()
    for copy in copies:
        copy.wait()


def expand(basis, other, mine, tiles=5):
    nx, _, cols = other.shape
    rows = basis.shape[0]
    return pl.pallas_call(
        functools.partial(expand_kernel, tiles),
        in_specs=[whole(), whole(), whole()],
        out_specs=pl.BlockSpec(memory_space=pl.ANY),
        out_shape=jax.ShapeDtypeStruct((rows, nx * cols), BF16),
        scratch_shapes=[pltpu.VMEM((rows, nx * cols), BF16), pltpu.SemaphoreType.DMA((tiles,))],
        compiler_params=pltpu.CompilerParams(vmem_limit_bytes=24 * 1024 * 1024),
    )(basis, other, mine)


def per_device(ny, nz, nx, inputs, out_grad, basis, moment_first, moment_second):
    rank = basis.shape[1]
    tokens = inputs.shape[0]
    groups = ny * nz
    own, cols = moment_first.shape
    half = rank // 2
    swap = [(0, 1), (1, 0)]

    theirs = lax.ppermute(out_grad, "c", swap)
    picks = rank_order(rank, own, ny, nz)
    parts = lax.all_to_all(project(inputs, basis, picks, nx), ("x", "c"), 0, 0)
    sums, theirs = lax.optimization_barrier((combine(parts), theirs))
    rows = lax.all_to_all(sums, "x", 0, 0)
    chip = project_grad(rows, out_grad, theirs).reshape(groups, own, cols)
    grad_shard, direction = direction_of(
        lax.all_to_all(chip, PLANE, 0, 0, axis_index_groups=plane_groups(ny, nz, [(0, 1)])), moment_first, moment_second, groups // 2
    )
    gathered = lax.all_to_all(direction, ("y", "zh"), 0, 0).reshape(half // 2, cols)
    mine, grad_shard = lax.optimization_barrier((spread(gathered, ("x", "zl"), 2 * nx), grad_shard))
    mine = mine.reshape(nx, half, cols)

    other = lax.ppermute(mine, "c", swap)
    new_first = 0.9 * moment_first + 0.1 * grad_shard
    new_second = 0.999 * moment_second + 0.001 * grad_shard * grad_shard
    done, ordered = expand_mine(basis, picks, mine)
    return (expand(ordered, other, done), new_first, new_second)


def solution(mesh):
    ny, nz, nx = 8, 8, mesh.devices.shape[1]
    split = Mesh(mesh.devices.reshape(ny, nz // 2, 2, 2, nx), ("y", "zh", "zl", "c", "x"))
    dp = ("y", "zh", "zl", "c")

    def body(*args):
        return per_device(ny, nz, nx, *args)

    return jax.shard_map(
        body,
        mesh=split,
        in_specs=(P(dp, "x"), P(dp, "x"), P("x", None), P(dp, "x"), P(dp, "x")),
        out_specs=(P("x", None), P(dp, "x"), P(dp, "x")),
        check_vma=False,
    )
```

```python
import functools

import jax
import jax.numpy as jnp
from jax import lax
from jax.experimental import pallas as pl
from jax.experimental.pallas import tpu as pltpu
from jax.sharding import Mesh, PartitionSpec as P

STEP = 10
MIRRORED = 1
F32 = jnp.float32
BF16 = jnp.bfloat16
PLANE = ("y", "zh", "zl", "c")


def spread(block, axes, n):
    return lax.all_to_all(jnp.broadcast_to(block[None], (n,) + block.shape), axes, 0, 0)


def whole():
    return pl.BlockSpec(memory_space=pltpu.VMEM)


def order_kernel(own, ny, nz, out_ref):
    _, rank, half = out_ref.shape
    old = lax.broadcasted_iota(jnp.int32, (rank, half), 0)
    new = lax.broadcasted_iota(jnp.int32, (rank, half), 1)
    block = new // own
    pair = block % (nz // 2)
    y = block // (nz // 2) % ny
    parity = block // (nz // 2 * ny)
    first = ((y * nz + pair * 2 + parity) * 2) * own + new % own
    turned_y, turned_pair = block % ny, block // ny % (nz // 2)
    mirrored = (((ny - 1 - turned_y) * nz + (nz // 2 - 1 - turned_pair) * 2 + parity) * 2) * own + new % own
    for c in range(2):
        start = mirrored if c == MIRRORED else first
        out_ref[c] = (old == start + c * own).astype(F32).astype(BF16)


def plane_groups(ny, nz, parities):
    pairs = nz // 2
    groups = []
    for some in parities:
        for c in range(2):
            order = [(p, y, z) for p in some for y in range(ny) for z in range(pairs)]
            if c == MIRRORED:
                order = [(p, ny - 1 - y, pairs - 1 - z) for p in some for z in range(pairs) for y in range(ny)]
            groups.append([((y * pairs + z) * 2 + p) * 2 + c for p, y, z in order])
    return groups


def rank_order(rank, own, ny, nz):
    return pl.pallas_call(
        functools.partial(order_kernel, own, ny, nz),
        in_specs=[],
        out_specs=whole(),
        out_shape=jax.ShapeDtypeStruct((2, rank, rank // 2), BF16),
        compiler_params=pltpu.CompilerParams(vmem_limit_bytes=16 * 1024 * 1024),
        cost_estimate=pl.CostEstimate(flops=4 * 10**9, bytes_accessed=8 * 10**6, transcendentals=0),
    )()


def project_kernel(inputs_ref, basis_ref, picks_ref, out_ref):
    size = out_ref.shape[1]
    part = jnp.dot(inputs_ref[...], basis_ref[...], preferred_element_type=F32).astype(BF16)
    for c in range(2):
        side = jnp.dot(part, picks_ref[c], preferred_element_type=F32).astype(BF16)
        for i in range(out_ref.shape[0] // 2):
            out_ref[2 * i + c] = side[i * size : (i + 1) * size]


def project(inputs, basis, picks, nx):
    tokens = inputs.shape[0]
    return pl.pallas_call(
        project_kernel,
        in_specs=[whole(), whole(), whole()],
        out_specs=whole(),
        out_shape=jax.ShapeDtypeStruct((2 * nx, tokens // nx, picks.shape[2]), BF16),
        compiler_params=pltpu.CompilerParams(vmem_limit_bytes=16 * 1024 * 1024),
    )(inputs, basis, picks)


def combine_kernel(parts_ref, out_ref):
    nx = out_ref.shape[0]
    for c in range(2):
        total = parts_ref[c].astype(F32)
        for i in range(1, nx):
            total += parts_ref[2 * i + c].astype(F32)
        total = total.astype(BF16)
        for i in range(nx):
            out_ref[i, c] = total


def combine(parts):
    both, tokens, half = parts.shape
    return pl.pallas_call(
        combine_kernel,
        in_specs=[whole()],
        out_specs=whole(),
        out_shape=jax.ShapeDtypeStruct((both // 2, 2, tokens, half), BF16),
        compiler_params=pltpu.CompilerParams(vmem_limit_bytes=16 * 1024 * 1024),
    )(parts)


def project_grad_kernel(rows_ref, own_ref, theirs_ref, out_ref):
    core = lax.axis_index("c")
    nx = rows_ref.shape[0]
    mine = jnp.concatenate([rows_ref[i, core] for i in range(nx)], axis=0)
    others = jnp.concatenate([rows_ref[i, 1 - core] for i in range(nx)], axis=0)
    total = lax.dot_general(
        mine, own_ref[...], (((0,), (0,)), ((), ())), preferred_element_type=F32
    )
    total += lax.dot_general(
        others, theirs_ref[...], (((0,), (0,)), ((), ())), preferred_element_type=F32
    )
    out_ref[...] = total.astype(BF16)


def project_grad(rows, own, theirs):
    return pl.pallas_call(
        project_grad_kernel,
        in_specs=[whole(), whole(), whole()],
        out_specs=whole(),
        out_shape=jax.ShapeDtypeStruct((rows.shape[3], own.shape[1]), BF16),
        compiler_params=pltpu.CompilerParams(vmem_limit_bytes=16 * 1024 * 1024),
    )(rows, own, theirs)


def direction_kernel(parts_ref, first_ref, second_ref, grad_ref, out_ref):
    grad = jnp.sum(parts_ref[...].astype(F32), axis=0)
    grad_ref[...] = grad
    new_first = 0.9 * first_ref[...] + 0.1 * grad
    new_second = 0.999 * second_ref[...] + 0.001 * grad * grad
    corrected = new_first / (1.0 - 0.9**STEP)
    scaled = jnp.sqrt(new_second / (1.0 - 0.999**STEP)) + 1e-08
    out_ref[...] = jnp.broadcast_to((corrected / scaled)[None], out_ref.shape).astype(BF16)


def direction_of(parts, first, second, peers):
    return pl.pallas_call(
        direction_kernel,
        in_specs=[whole(), whole(), whole()],
        out_specs=[whole(), whole()],
        out_shape=[
            jax.ShapeDtypeStruct(first.shape, F32),
            jax.ShapeDtypeStruct((peers,) + parts.shape[1:], BF16),
        ],
        compiler_params=pltpu.CompilerParams(vmem_limit_bytes=16 * 1024 * 1024),
    )(parts, first, second)


def expand_mine_kernel(basis_ref, picks_ref, mine_ref, out_ref, ordered_ref):
    nx, half, _ = mine_ref.shape
    core = lax.axis_index("c")
    for h in range(2):
        pick = picks_ref[core if h == 0 else 1 - core]
        ordered_ref[:, h * half : (h + 1) * half] = jnp.dot(
            basis_ref[...], pick, preferred_element_type=F32
        ).astype(BF16)
    for i in range(nx):
        out_ref[i] = jnp.dot(ordered_ref[:, :half], mine_ref[i], preferred_element_type=F32)


def expand_mine(basis, picks, mine):
    nx, half, cols = mine.shape
    rows = basis.shape[0]
    return pl.pallas_call(
        expand_mine_kernel,
        in_specs=[whole(), whole(), whole()],
        out_specs=[whole(), whole()],
        out_shape=[
            jax.ShapeDtypeStruct((nx, rows, cols), F32),
            jax.ShapeDtypeStruct(basis.shape, BF16),
        ],
        compiler_params=pltpu.CompilerParams(vmem_limit_bytes=24 * 1024 * 1024),
        cost_estimate=pl.CostEstimate(
            flops=2 * rows * half * nx * cols, bytes_accessed=4 * nx * rows * cols, transcendentals=0
        ),
    )(basis, picks, mine)


def expand_kernel(tiles, basis_ref, other_ref, mine_ref, out_ref, done, sems):
    nx, half, cols = other_ref.shape
    size = basis_ref.shape[0] // tiles
    copies = []
    for t in range(tiles):
        rows = pl.ds(t * size, size)
        for i in range(nx):
            acc = mine_ref[i, rows, :] + jnp.dot(
                basis_ref[rows, half:], other_ref[i], preferred_element_type=F32
            )
            done[rows, pl.ds(i * cols, cols)] = acc.astype(BF16)
        copies.append(pltpu.make_async_copy(done.at[rows], out_ref.at[rows], sems.at[t]))
        copies[-1].start()
    for copy in copies:
        copy.wait()


def expand(basis, other, mine, tiles=5):
    nx, _, cols = other.shape
    rows = basis.shape[0]
    return pl.pallas_call(
        functools.partial(expand_kernel, tiles),
        in_specs=[whole(), whole(), whole()],
        out_specs=pl.BlockSpec(memory_space=pl.ANY),
        out_shape=jax.ShapeDtypeStruct((rows, nx * cols), BF16),
        scratch_shapes=[pltpu.VMEM((rows, nx * cols), BF16), pltpu.SemaphoreType.DMA((tiles,))],
        compiler_params=pltpu.CompilerParams(vmem_limit_bytes=24 * 1024 * 1024),
    )(basis, other, mine)


def per_device(ny, nz, nx, inputs, out_grad, basis, moment_first, moment_second):
    rank = basis.shape[1]
    tokens = inputs.shape[0]
    groups = ny * nz
    own, cols = moment_first.shape
    half = rank // 2
    swap = [(0, 1), (1, 0)]

    theirs = lax.ppermute(out_grad, "c", swap)
    picks = rank_order(rank, own, ny, nz)
    parts = lax.all_to_all(project(inputs, basis, picks, nx), ("x", "c"), 0, 0)
    sums, theirs = lax.optimization_barrier((combine(parts), theirs))
    rows = lax.all_to_all(sums, "x", 0, 0)
    chip = project_grad(rows, out_grad, theirs).reshape(groups, own, cols)
    grad_shard, direction = direction_of(
        lax.all_to_all(chip, PLANE, 0, 0, axis_index_groups=plane_groups(ny, nz, [(0, 1)])), moment_first, moment_second, groups // 2
    )
    gathered = lax.all_to_all(
        direction, PLANE, 0, 0, axis_index_groups=plane_groups(ny, nz, [(0,), (1,)])
    ).reshape(half // 2, cols)
    mine, grad_shard = lax.optimization_barrier((spread(gathered, ("x", "zl"), 2 * nx), grad_shard))
    mine = mine.reshape(nx, half, cols)

    other = lax.ppermute(mine, "c", swap)
    new_first = 0.9 * moment_first + 0.1 * grad_shard
    new_second = 0.999 * moment_second + 0.001 * grad_shard * grad_shard
    done, ordered = expand_mine(basis, picks, mine)
    return (expand(ordered, other, done), new_first, new_second)


def solution(mesh):
    ny, nz, nx = 8, 8, mesh.devices.shape[1]
    split = Mesh(mesh.devices.reshape(ny, nz // 2, 2, 2, nx), ("y", "zh", "zl", "c", "x"))
    dp = ("y", "zh", "zl", "c")

    def body(*args):
        return per_device(ny, nz, nx, *args)

    return jax.shard_map(
        body,
        mesh=split,
        in_specs=(P(dp, "x"), P(dp, "x"), P("x", None), P(dp, "x"), P(dp, "x")),
        out_specs=(P("x", None), P(dp, "x"), P(dp, "x")),
        check_vma=False,
    )
```
